256 devices in a mesh: dp: 8 (over y, core), seq: 32 (over z, x).
Axes of the slice: x: 4, y: 4, z: 8, core: 2. Of those that a mesh axis runs over, the one named last changes fastest.
Arguments:
- queries: bfloat16 [8, 4096, 4096], P('dp', 'seq'), may hold values from -120 to 120, as said below
- keys: bfloat16 [8, 4096, 512], P('dp', 'seq'), may hold values from -4 to 4
- values: bfloat16 [8, 4096, 512], P('dp', 'seq'), may hold values from -6 to 6
- cotangent: bfloat16 [8, 4096, 4096], P('dp', 'seq'), may hold values from -6 to 6
- lengths: int32 [8, 16], P('dp'), may hold values from 1 to 1024, 4096 in all within a row
- loss_mask: int32 [8, 4096], P('dp', 'seq'), may hold values from 0 to 1, as said below
Outputs:
- attn_out: bfloat16 [8, 4096, 4096], P('dp', 'seq')
- grad_q: bfloat16 [8, 4096, 4096], P('dp', 'seq')
- grad_k: bfloat16 [8, 4096, 512], P('dp', 'seq')
- grad_v: bfloat16 [8, 4096, 512], P('dp', 'seq')
- row_loss: float32 [8], P('dp')
The draws below stay inside these ranges and needn't reach their ends.
Inputs may be any that keep to these rules, and one draw needn't show every extreme that they name: `queries`: in the shown draw entries lie within -4 to 4. Each row's 16 lengths sum to 4096; the longest is exactly 1024. `loss_mask`: entries are 0 or 1; position 0 of every row is 1.
All inputs are finite; a program needn't handle non-finite values.
Results may differ from the reference program's by a relative error of at most 0.015.
The reference program's roundings to bfloat16 on the way (of `probs`, `upstream` and `score_grad`) count: a program that leaves them out, or rounds other values in their place, can miss the bound.
Values may be sent and summed in bfloat16 or wider, within the bound.
No kernel may reach another device: no remote copies, remote signals or barrier semaphores. Data moves between devices by JAX's collectives and lax.ppermute only.
A program may use at most 64 MiB of HBM per device.

```python
import math
import jax
import jax.numpy as jnp
import numpy as np
from jax import lax

HD = 128
GROUP = 8
NDOC = 16
QH = 32
KVH = 4
SEQ_LEN = 4096
ROWS = 8
DOC_MOST = 1024


def shared_keys(key):
    base = jax.random.normal(key, (ROWS, SEQ_LEN, KVH, HD), jnp.float32)
    return jnp.clip(base, -4.0, 4.0)


def draw_keys(key, part):
    base = shared_keys(key)
    return base.reshape(ROWS, SEQ_LEN, KVH * HD).astype(jnp.bfloat16)


def draw_queries(key, part):
    key = jax.random.fold_in(key, 12)
    fresh = jnp.clip(jax.random.normal(key, (ROWS, SEQ_LEN, QH, HD), jnp.float32), -4.0, 4.0)
    return fresh.reshape(ROWS, SEQ_LEN, QH * HD).astype(jnp.bfloat16)


def draw_loss_mask(key, part):
    key = jax.random.fold_in(key, 5)
    row_index = jnp.arange(ROWS, dtype=jnp.int32)[:, None]
    positions = jnp.arange(SEQ_LEN, dtype=jnp.int32)[None, :]
    level = 300 + 600 * (row_index * SEQ_LEN + positions) // (ROWS * SEQ_LEN)
    rolled = jax.random.randint(key, (ROWS, SEQ_LEN), 0, 1000, dtype=jnp.int32)
    valid = (rolled < level) | (positions == 0)
    return valid.astype(jnp.int32)


def block_scale(stream_key, dims, pieces, smallest, top_value):
    gain = 1.0
    for axis_at, shards_of in pieces:
        steps = jax.random.uniform(jax.random.fold_in(jax.random.fold_in(stream_key, 6), axis_at), (shards_of,), jnp.float32, smallest / len(pieces), top_value / len(pieces))
        gain = gain * jnp.repeat(jnp.exp(steps), dims[axis_at] // shards_of).reshape((-1,) + (1,) * (len(dims) - 1 - axis_at))
    return gain


def length_profile(number_of, total, bound, lean):
    weights = [(1 << 20) // math.isqrt(rank ** lean) + 1 for rank in range(2, number_of + 1)]
    spare, holding = total - bound - (number_of - 1), [1] * (number_of - 1)
    while spare > 0:
        candidates = [i for i in range(number_of - 1) if holding[i] < bound]
        pool, budget = sum([weights[i] for i in candidates]), spare
        for i in candidates:
            more = min(bound - holding[i], max(1, budget * weights[i] // pool), spare)
            holding[i] = holding[i] + more
            spare = spare - more
    return np.array([bound] + holding)


def ragged(own_key, number_of, total, limit, slope):
    if number_of == 2:
        one = jax.random.randint(own_key, (), max(1, total - limit), min(limit, total - 1) + 1)
        return jnp.stack([one, total - one])
    tallies = jnp.asarray(length_profile(number_of, total, limit, slope), jnp.int32)
    twos = (number_of - 1) // 2
    donor, receiver = tallies[1:1 + 2 * twos:2], tallies[2:2 + 2 * twos:2]
    room = jnp.minimum(donor - 1, limit - receiver)
    shifted = jax.random.randint(jax.random.fold_in(own_key, 1), (twos,), 0, 1 << 20) % (room + 1)
    tallies = tallies.at[1:1 + 2 * twos:2].set(donor - shifted).at[2:2 + 2 * twos:2].set(receiver + shifted)
    return tallies[jax.random.permutation(jax.random.fold_in(own_key, 2), number_of)]


def gaussian(own_key, extent, deviation, reach, shards=(), kind=jnp.bfloat16):
    level = block_scale(own_key, extent, shards, -0.22, 0.18) if shards else 1.0
    drawn = jax.random.normal(own_key, extent, jnp.float32) * deviation * level
    return jnp.minimum(jnp.maximum(drawn, -reach), reach).astype(kind)


def setup_inputs(seed: int = 0) -> dict:
    arg_keys = jax.random.split(jax.random.key(seed), 7)
    queries = draw_queries(jax.random.fold_in(arg_keys[6], 71), 0)
    keys = draw_keys(jax.random.fold_in(arg_keys[6], 71), 0)
    values = gaussian(arg_keys[2], (ROWS, SEQ_LEN, KVH * HD), 1.0, 6.0, ((0, 8), (1, 32)))
    cotangent = gaussian(arg_keys[3], (ROWS, SEQ_LEN, QH * HD), 1.0, 6.0, ((0, 8), (1, 32)))
    lengths = jax.vmap(lambda own: ragged(own, NDOC, SEQ_LEN, DOC_MOST, 2))(jax.random.split(arg_keys[4], ROWS)).reshape((ROWS, NDOC)).astype(jnp.int32)
    loss_mask = draw_loss_mask(jax.random.fold_in(arg_keys[6], 71), 0)
    return dict(queries=queries, keys=keys, values=values, cotangent=cotangent, lengths=lengths, loss_mask=loss_mask)


masked_value = -1.0e30


def document_index(lengths_row):
    doc_ends = jnp.cumsum(lengths_row)
    doc_starts = doc_ends - lengths_row
    positions = jnp.arange(SEQ_LEN, dtype=jnp.int32)
    return jnp.sum((positions[:, None] >= doc_starts[None, :]).astype(jnp.int32), axis=1)


def head_pass(query_head, key_head, value_head, upstream_head, allowed, key_factor, value_factor):
    score_scale = HD ** -0.5
    scores = jnp.dot(query_head, key_head.T, preferred_element_type=jnp.float32) * score_scale
    scores = jnp.where(allowed, scores, masked_value)
    row_top = jnp.max(scores, axis=1)
    log_total = row_top + jnp.log(jnp.sum(jnp.where(allowed, jnp.exp(scores - row_top[:, None]), 0.0), axis=1))
    weights = jnp.where(allowed, jnp.exp(scores - log_total[:, None]), 0.0)
    probs = weights.astype(jnp.bfloat16)
    output = jnp.dot(probs, value_head, preferred_element_type=jnp.float32).astype(jnp.bfloat16)
    delta = jnp.sum(upstream_head.astype(jnp.float32) * output.astype(jnp.float32), axis=1)
    prob_grad = jnp.dot(upstream_head, value_head.T, preferred_element_type=jnp.float32)
    score_grad = (weights * (prob_grad - delta[:, None])).astype(jnp.bfloat16)
    grad_query = (key_factor * jnp.dot(score_grad, key_head, preferred_element_type=jnp.float32)).astype(jnp.bfloat16)
    key_part = (key_factor * jnp.dot(score_grad.T, query_head, preferred_element_type=jnp.float32)).astype(jnp.bfloat16)
    value_part = (value_factor * jnp.dot(probs.T, upstream_head, preferred_element_type=jnp.float32)).astype(jnp.bfloat16)
    return output, grad_query, key_part, value_part


def reference(queries, keys, values, cotangent, lengths, loss_mask):
    token_total = jnp.sum(loss_mask).astype(jnp.float32)
    grad_scale = jnp.float32(ROWS * SEQ_LEN) / token_total
    key_factor = grad_scale * (HD ** -0.5)
    positions = jnp.arange(SEQ_LEN, dtype=jnp.int32)
    outputs, query_grads, key_grads, value_grads, losses = [], [], [], [], []
    for row in range(ROWS):
        doc = document_index(lengths[row])
        allowed = (doc[:, None] == doc[None, :]) & (positions[None, :] <= positions[:, None])
        upstream = jnp.where(loss_mask[row][:, None] > 0, cotangent[row], 0).astype(jnp.bfloat16)
        query_split = queries[row].reshape(SEQ_LEN, KVH, GROUP, HD).transpose(1, 2, 0, 3)
        upstream_split = upstream.reshape(SEQ_LEN, KVH, GROUP, HD).transpose(1, 2, 0, 3)
        key_split = keys[row].reshape(SEQ_LEN, KVH, HD).transpose(1, 0, 2)
        value_split = values[row].reshape(SEQ_LEN, KVH, HD).transpose(1, 0, 2)

        def per_group(items):
            query_group, key_head, value_head, upstream_group = items
            group_out, group_dq = [], []
            key_sum = jnp.zeros((SEQ_LEN, HD), jnp.float32)
            value_sum = jnp.zeros((SEQ_LEN, HD), jnp.float32)
            for member in range(GROUP):
                output, grad_query, key_part, value_part = head_pass(
                    query_group[member], key_head, value_head, upstream_group[member], allowed, key_factor, grad_scale)
                group_out.append(output)
                group_dq.append(grad_query)
                key_sum = key_sum + key_part.astype(jnp.float32)
                value_sum = value_sum + value_part.astype(jnp.float32)
            return (jnp.stack(group_out), jnp.stack(group_dq), key_sum.astype(jnp.bfloat16), value_sum.astype(jnp.bfloat16))

        output, grad_query, grad_key, grad_value = lax.map(per_group, (query_split, key_split, value_split, upstream_split))
        output = output.transpose(2, 0, 1, 3).reshape(SEQ_LEN, QH * HD)
        outputs.append(output)
        query_grads.append(grad_query.transpose(2, 0, 1, 3).reshape(SEQ_LEN, QH * HD))
        key_grads.append(grad_key.transpose(1, 0, 2).reshape(SEQ_LEN, KVH * HD))
        value_grads.append(grad_value.transpose(1, 0, 2).reshape(SEQ_LEN, KVH * HD))
        token_terms = jnp.sum(output.astype(jnp.float32) * cotangent[row].astype(jnp.float32), axis=1)
        row_sum = jnp.sum(loss_mask[row].astype(jnp.float32) * token_terms)
        losses.append(grad_scale * row_sum / SEQ_LEN)
    return (jnp.stack(outputs), jnp.stack(query_grads), jnp.stack(key_grads), jnp.stack(value_grads), jnp.stack(losses))
```

```python
import functools
import math

import jax
import jax.numpy as jnp
from jax import lax
from jax.experimental import pallas as pl
from jax.experimental.pallas import tpu as pltpu
from jax.sharding import PartitionSpec as P

HD = 128
GROUP = 8
RING = 4
SLOTS = 9
MASKED = -1e30
EXP2_SCALE = HD ** -0.5 * math.log2(math.e)
STRIP = 64

NT = (((1,), (1,)), ((), ()))
NN = (((1,), (0,)), ((), ()))
TN = (((0,), (0,)), ((), ()))


def mxu(a, b, dims):
    return lax.dot_general(a, b, dims, preferred_element_type=jnp.float32)


def attend_kernel(
    block_of, lengths, factor, q_ref, c_ref, mask_ref, kv_ref,
    out_ref, dq_ref, dkv_ref, loss_ref,
    bias, valid, kg, vg, score, prob, sgrad, dk, dv,
):
    tok = q_ref.shape[0]
    kv_width = kv_ref.shape[2] // 2
    slots = kv_ref.shape[0]
    strips = slots * tok // STRIP
    pos = block_of[0] * tok + lax.broadcasted_iota(jnp.int32, (1, tok), 1)
    first = jnp.zeros((1, tok), jnp.int32)
    start = jnp.int32(0)
    for j in range(lengths.shape[1]):
        first = jnp.where(pos >= start, start, first)
        start = start + lengths[0, j]
    for j in range(slots):
        key_pos = block_of[j] * tok + lax.broadcasted_iota(jnp.int32, (tok, tok), 0)
        allowed = (key_pos >= first) & (key_pos <= pos)
        bias[j * tok:(j + 1) * tok, :] = jnp.where(allowed, 0.0, MASKED)
    mask_rows = jnp.broadcast_to(mask_ref[...].astype(jnp.float32), (tok, tok))
    valid[...] = mask_rows.T.astype(jnp.bfloat16)
    loss_ref[...] = jnp.zeros_like(loss_ref)

    def group_step(g, _):
        k_at = pl.multiple_of(g * HD, HD)
        v_at = pl.multiple_of(g * HD + kv_width, HD)
        for j in range(slots):
            kg[j * tok:(j + 1) * tok, :] = kv_ref[j, :, pl.ds(k_at, HD)]
            vg[j * tok:(j + 1) * tok, :] = kv_ref[j, :, pl.ds(v_at, HD)]
        dk[...] = jnp.zeros_like(dk)
        dv[...] = jnp.zeros_like(dv)

        def head_pair_step(pair, _):
            h0 = pl.multiple_of((g * GROUP + 2 * pair) * HD, HD)
            h1 = pl.multiple_of((g * GROUP + 2 * pair + 1) * HD, HD)
            q = jnp.concatenate([q_ref[:, pl.ds(h0, HD)], q_ref[:, pl.ds(h1, HD)]], axis=0)
            up = jnp.concatenate(
                [c_ref[:, pl.ds(h0, HD)] * valid[...], c_ref[:, pl.ds(h1, HD)] * valid[...]],
                axis=0,
            )
            wide = 2 * tok
            score[...] = mxu(kg[...], q, NT)
            top = jnp.full((8, wide), MASKED, jnp.float32)
            for j in range(strips):
                at = slice(j * STRIP, (j + 1) * STRIP)
                b = bias[at, :]
                s = score[at, :] + jnp.concatenate([b, b], axis=1)
                score[at, :] = s
                top = jnp.maximum(top, jnp.max(s.reshape(STRIP // 8, 8, wide), axis=0))
            top = jnp.max(top, axis=0, keepdims=True)
            total = jnp.zeros((8, wide), jnp.float32)
            for j in range(strips):
                at = slice(j * STRIP, (j + 1) * STRIP)
                e = jnp.exp2((score[at, :] - top) * EXP2_SCALE)
                score[at, :] = e
                total = total + jnp.sum(e.reshape(STRIP // 8, 8, wide), axis=0)
            inverse = 1.0 / jnp.sum(total, axis=0, keepdims=True)
            for j in range(strips):
                at = slice(j * STRIP, (j + 1) * STRIP)
                w = score[at, :] * inverse
                score[at, :] = w
                prob[at, :] = w.astype(jnp.bfloat16)
            out_t = mxu(vg[...], prob[...], TN).astype(jnp.bfloat16)
            out = out_t.T
            out_ref[:, pl.ds(h0, HD)] = out[:tok]
            out_ref[:, pl.ds(h1, HD)] = out[tok:]
            up_t = up.T
            terms = up_t.astype(jnp.float32) * out_t.astype(jnp.float32)
            delta = jnp.sum(terms, axis=0, keepdims=True)
            loss_ref[...] += delta[:, :tok] + delta[:, tok:]
            pgrad = mxu(vg[...], up_t, NN)
            for j in range(strips):
                at = slice(j * STRIP, (j + 1) * STRIP)
                sgrad[at, :] = (score[at, :] * (pgrad[at, :] - delta)).astype(jnp.bfloat16)
            dq = (mxu(kg[...], sgrad[...], TN) * factor[0, 0]).astype(jnp.bfloat16).T
            dq_ref[:, pl.ds(h0, HD)] = dq[:tok]
            dq_ref[:, pl.ds(h1, HD)] = dq[tok:]
            dk[...] += mxu(sgrad[...], q, NN)
            dv[...] += mxu(prob[...], up, NN)
            return 0

        lax.fori_loop(0, GROUP // 2, head_pair_step, 0)
        for j in range(slots):
            at = slice(j * tok, (j + 1) * tok)
            dkv_ref[j, :, pl.ds(k_at, HD)] = dk[at, :].astype(jnp.bfloat16)
            dkv_ref[j, :, pl.ds(v_at, HD)] = dv[at, :].astype(jnp.bfloat16)
        return 0

    lax.fori_loop(0, kv_width // HD, group_step, 0)


def attend(block_of, lengths, factor, queries, cotangent, mask, kv):
    tok = queries.shape[0]
    rows = kv.shape[0] * tok
    vmem = pl.BlockSpec(memory_space=pltpu.VMEM)
    smem = pl.BlockSpec(memory_space=pltpu.SMEM)
    f32, bf16 = jnp.float32, jnp.bfloat16
    return pl.pallas_call(
        attend_kernel,
        out_shape=(
            jax.ShapeDtypeStruct(queries.shape, bf16),
            jax.ShapeDtypeStruct(queries.shape, bf16),
            jax.ShapeDtypeStruct(kv.shape, bf16),
            jax.ShapeDtypeStruct((1, tok), f32),
        ),
        in_specs=[smem, smem, smem, vmem, vmem, vmem, vmem],
        out_specs=(vmem, vmem, vmem, vmem),
        scratch_shapes=[
            pltpu.VMEM((rows, tok), f32),
            pltpu.VMEM((tok, tok), bf16),
            pltpu.VMEM((rows, HD), bf16),
            pltpu.VMEM((rows, HD), bf16),
            pltpu.VMEM((rows, 2 * tok), f32),
            pltpu.VMEM((rows, 2 * tok), bf16),
            pltpu.VMEM((rows, 2 * tok), bf16),
            pltpu.VMEM((rows, HD), f32),
            pltpu.VMEM((rows, HD), f32),
        ],
        compiler_params=pltpu.CompilerParams(vmem_limit_bytes=48 * 2**20),
    )(block_of, lengths, factor, queries, cotangent, mask, kv)


def per_device(queries, keys, values, cotangent, lengths, loss_mask):
    seq_count = lax.axis_size("seq")
    dp_count = lax.axis_size("dp")
    tok = queries.shape[1]
    kv_width = keys.shape[2]
    me = lax.axis_index("seq")
    x = lax.rem(me, RING)

    def down(step):
        return [(i, i + step) for i in range(seq_count - step)]

    def up(step):
        return [(i + step, i) for i in range(seq_count - step)]

    def around(step):
        return [(i, i - i % RING + (i + step) % RING) for i in range(seq_count)]

    mask_all = lax.all_gather(loss_mask.astype(jnp.float32), ("dp", "seq"))
    own = jnp.concatenate([keys[0], values[0]], axis=1)
    near = lax.ppermute(own, "seq", down(RING))
    far = lax.ppermute(own, "seq", down(2 * RING))
    got = []
    for step in range(1, RING):
        send = jnp.stack([jnp.where(x + step >= RING, far, own), near])
        got.append(lax.ppermute(send, "seq", around(step)))
    steps = jnp.arange(1, RING, dtype=jnp.int32)
    inside = x >= steps
    block_of = jnp.concatenate([
        jnp.stack([me, me - RING, me - 2 * RING]),
        jnp.where(inside, me - steps, me - RING - steps),
        jnp.where(inside, me - RING - steps, me - steps),
    ]).astype(jnp.int32)
    kv = jnp.stack([own, near, far] + [g[0] for g in got] + [g[1] for g in got])
    token_total = jnp.sum(mask_all)
    grad_scale = jnp.float32(dp_count * seq_count * tok) / token_total
    factor = (grad_scale * HD ** -0.5).reshape(1, 1)
    out, dq, dkv, loss = attend(
        block_of, lengths, factor, queries[0], cotangent[0], loss_mask, kv
    )
    loss_all = lax.all_gather(loss, ("dp", "seq"))
    loss_row = lax.dynamic_index_in_dim(
        loss_all.reshape(dp_count, seq_count * tok), lax.axis_index("dp"), 0, keepdims=False
    )
    row_loss = (grad_scale * jnp.sum(loss_row) / (seq_count * tok)).reshape(1)

    own_sum = dkv[0].astype(jnp.float32)
    near_sum = dkv[1].astype(jnp.float32)
    far_sum = dkv[2].astype(jnp.float32)
    back = [
        lax.ppermute(jnp.stack([dkv[2 + d], dkv[5 + d]]), "seq", around(-d))
        for d in range(1, RING)
    ]
    for d in range(1, RING):
        part = back[d - 1][0].astype(jnp.float32)
        near_sum = near_sum + back[d - 1][1].astype(jnp.float32)
        own_sum = own_sum + jnp.where(x + d < RING, part, 0.0)
        far_sum = far_sum + jnp.where(x + d < RING, 0.0, part)
    near_back = lax.ppermute(near_sum.astype(jnp.bfloat16), "seq", up(RING))
    far_back = lax.ppermute(far_sum.astype(jnp.bfloat16), "seq", up(2 * RING))
    total = own_sum + near_back.astype(jnp.float32) + far_back.astype(jnp.float32)
    grad_k = (total[:, :kv_width] * factor[0, 0]).astype(jnp.bfloat16)
    grad_v = (total[:, kv_width:] * grad_scale).astype(jnp.bfloat16)
    return (out[None], dq[None], grad_k[None], grad_v[None], row_loss)


def solution(mesh):
    return jax.shard_map(
        per_device,
        mesh=mesh,
        in_specs=(
            P("dp", "seq", None),
            P("dp", "seq", None),
            P("dp", "seq", None),
            P("dp", "seq", None),
            P("dp", None),
            P("dp", "seq"),
        ),
        out_specs=(
            P("dp", "seq", None),
            P("dp", "seq", None),
            P("dp", "seq", None),
            P("dp", "seq", None),
            P("dp"),
        ),
        check_vma=False,
    )
```

```python
import functools
import math

import jax
import jax.numpy as jnp
from jax import lax
from jax.experimental import pallas as pl
from jax.experimental.pallas import tpu as pltpu
from jax.sharding import PartitionSpec as P

HD = 128
GROUP = 8
RING = 4
ORDER = (1, 3, 2)
SLOTS = 3 + 2 * len(ORDER)
PARTS = ((0, 2), (2, 2))
MASKED = -1e30
EXP2_SCALE = HD ** -0.5 * math.log2(math.e)
EXTRA = 16
STRIP = 64

NT = (((1,), (1,)), ((), ()))
NN = (((1,), (0,)), ((), ()))
TN = (((0,), (0,)), ((), ()))


def mxu(a, b, dims):
    return lax.dot_general(a, b, dims, preferred_element_type=jnp.float32)


def attend_kernel(block_of, lengths, q_ref, c_ref, mask_ref, count_ref, loss_in, *refs):
    n = len(ORDER)
    key_refs, value_refs = refs[:SLOTS], refs[SLOTS:2 * SLOTS]
    out_ref, dq_ref, loss_ref = refs[2 * SLOTS:2 * SLOTS + 3]
    refs = refs[2 * SLOTS + 3:]
    single_grads, pair_grads = refs[:3], refs[3:3 + n]
    bias, valid, kg, vg, score, prob, sgrad, dk, dv = refs[3 + n:]
    tok = q_ref.shape[0]
    halves = [slice(0, tok), slice(tok, 2 * tok)]
    grads = [r.at[...] for r in single_grads] + [r.at[h] for h in halves for r in pair_grads]
    strips = SLOTS * tok // STRIP

    @pl.when(pl.program_id(0) == 0)
    def _():
        pos = block_of[0] * tok + lax.broadcasted_iota(jnp.int32, (1, tok), 1)
        first = jnp.zeros((1, tok), jnp.int32)
        start = jnp.int32(0)
        for j in range(lengths.shape[1]):
            first = jnp.where(pos >= start, start, first)
            start = start + lengths[0, j]
        for j in range(SLOTS):
            key_pos = block_of[j] * tok + lax.broadcasted_iota(jnp.int32, (tok, tok), 0)
            allowed = (key_pos >= first) & (key_pos <= pos)
            bias[j * tok:(j + 1) * tok, :] = jnp.where(allowed, 0.0, MASKED)
        mask_rows = jnp.broadcast_to(mask_ref[...].astype(jnp.float32), (tok, tok))
        valid[...] = mask_rows.T.astype(jnp.bfloat16)
        loss_ref[...] = loss_in[...]

    for j in range(SLOTS):
        kg[j * tok:(j + 1) * tok, :] = key_refs[j][...]
        vg[j * tok:(j + 1) * tok, :] = value_refs[j][...]
    dk[...] = jnp.zeros_like(dk)
    dv[...] = jnp.zeros_like(dv)

    def head_pair_step(pair, _):
        h0 = pl.multiple_of(2 * pair * HD, HD)
        h1 = pl.multiple_of((2 * pair + 1) * HD, HD)
        q = jnp.concatenate([q_ref[:, pl.ds(h0, HD)], q_ref[:, pl.ds(h1, HD)]], axis=0)
        up = jnp.concatenate(
            [c_ref[:, pl.ds(h0, HD)] * valid[...], c_ref[:, pl.ds(h1, HD)] * valid[...]],
            axis=0,
        )
        wide = 2 * tok
        score[...] = mxu(kg[...], q, NT)
        top = jnp.full((8, wide), MASKED, jnp.float32)
        for j in range(strips):
            at = slice(j * STRIP, (j + 1) * STRIP)
            b = bias[at, :]
            s = score[at, :] + jnp.concatenate([b, b], axis=1)
            score[at, :] = s
            top = jnp.maximum(top, jnp.max(s.reshape(STRIP // 8, 8, wide), axis=0))
        top = jnp.max(top, axis=0, keepdims=True)
        total = jnp.zeros((8, wide), jnp.float32)
        for j in range(strips):
            at = slice(j * STRIP, (j + 1) * STRIP)
            e = jnp.exp2((score[at, :] - top) * EXP2_SCALE)
            score[at, :] = e
            total = total + jnp.sum(e.reshape(STRIP // 8, 8, wide), axis=0)
        inverse = 1.0 / jnp.sum(total, axis=0, keepdims=True)
        for j in range(strips):
            at = slice(j * STRIP, (j + 1) * STRIP)
            w = score[at, :] * inverse
            score[at, :] = w
            prob[at, :] = w.astype(jnp.bfloat16)
        out_t = mxu(vg[...], prob[...], TN).astype(jnp.bfloat16)
        out = out_t.T
        out_ref[:, pl.ds(h0, HD)] = out[:tok]
        out_ref[:, pl.ds(h1, HD)] = out[tok:]
        up_t = up.T
        terms = up_t.astype(jnp.float32) * out_t.astype(jnp.float32)
        delta = jnp.sum(terms, axis=0, keepdims=True)
        loss_ref[...] += delta[:, :tok] + delta[:, tok:]
        pgrad = mxu(vg[...], up_t, NN)
        for j in range(strips):
            at = slice(j * STRIP, (j + 1) * STRIP)
            sgrad[at, :] = (score[at, :] * (pgrad[at, :] - delta)).astype(jnp.bfloat16)
        dq = mxu(kg[...], sgrad[...], TN).T
        dq_ref[:, pl.ds(h0, HD)] = dq[:tok]
        dq_ref[:, pl.ds(h1, HD)] = dq[tok:]
        dk[...] += mxu(sgrad[...], q, NN)
        dv[...] += mxu(prob[...], up, NN)
        return 0

    lax.fori_loop(0, GROUP // 2, head_pair_step, 0)
    for j in range(SLOTS):
        at = slice(j * tok, (j + 1) * tok)
        grads[j][:, :HD] = dk[at, :].astype(jnp.bfloat16)
        grads[j][:, HD:] = dv[at, :].astype(jnp.bfloat16)
    if pair_grads[0].shape[0] == 2 * tok:
        return

    high = loss_ref[...].astype(jnp.bfloat16).astype(jnp.float32)
    middle = (loss_ref[...] - high).astype(jnp.bfloat16).astype(jnp.float32)
    low = loss_ref[...] - high - middle
    row_of = lax.broadcasted_iota(jnp.int32, (EXTRA, tok), 0)
    extra = jnp.zeros((EXTRA, tok), jnp.float32)
    for i, row in enumerate([high, middle, low, count_ref[...]]):
        extra = jnp.where(row_of == i, row, extra)
    for ref in pair_grads:
        ref[2 * tok:, :HD] = extra.astype(jnp.bfloat16)
        ref[2 * tok:, HD:] = extra.astype(jnp.bfloat16)


def attend(part, block_of, lengths, queries, cotangent, mask, counts, loss, blocks):
    first_head, heads = part
    tok = queries.shape[0]
    kv_heads = blocks[0].shape[1] // (2 * HD)
    wide = GROUP * HD
    rows = SLOTS * tok
    n = len(ORDER)
    f32, bf16 = jnp.float32, jnp.bfloat16
    smem = pl.BlockSpec(memory_space=pltpu.SMEM)
    row = pl.BlockSpec((1, tok), lambda g: (0, 0))
    wide_in = pl.BlockSpec((tok, wide), lambda g: (0, first_head + g))
    wide_out = pl.BlockSpec((tok, wide), lambda g: (0, g))
    key = pl.BlockSpec((tok, HD), lambda g: (0, first_head + g))
    value = pl.BlockSpec((tok, HD), lambda g: (0, kv_heads + first_head + g))
    single = pl.BlockSpec((tok, 2 * HD), lambda g: (0, g))
    pair_rows = 2 * tok + (EXTRA if part is PARTS[-1] else 0)
    pair = pl.BlockSpec((pair_rows, 2 * HD), lambda g: (0, g))
    halo = [key] * SLOTS + [value] * SLOTS
    grads = [pltpu.HBM((tok, heads * 2 * HD), bf16)] * 3
    grads += [pltpu.HBM((pair_rows, heads * 2 * HD), bf16)] * n
    work = 12 * heads * GROUP * tok * rows * HD
    result = pl.pallas_call(
        attend_kernel,
        grid=(heads,),
        out_shape=(
            pltpu.HBM((tok, heads * wide), bf16),
            pltpu.HBM((tok, heads * wide), f32),
            jax.ShapeDtypeStruct((1, tok), f32),
            *grads,
        ),
        in_specs=[smem, smem, wide_in, wide_in, row, row, row, *halo],
        out_specs=(wide_out, wide_out, row, *[single] * 3, *[pair] * n),
        scratch_shapes=[
            pltpu.VMEM((rows, tok), f32),
            pltpu.VMEM((tok, tok), bf16),
            pltpu.VMEM((rows, HD), bf16),
            pltpu.VMEM((rows, HD), bf16),
            pltpu.VMEM((rows, 2 * tok), f32),
            pltpu.VMEM((rows, 2 * tok), bf16),
            pltpu.VMEM((rows, 2 * tok), bf16),
            pltpu.VMEM((rows, HD), f32),
            pltpu.VMEM((rows, HD), f32),
        ],
        compiler_params=pltpu.CompilerParams(vmem_limit_bytes=16 * 2**20),
        cost_estimate=pl.CostEstimate(
            flops=2 * work, bytes_accessed=8 * 2**20, transcendentals=work // (12 * HD)
        ),
    )(block_of, lengths, queries, cotangent, mask, counts, loss, *blocks, *blocks)
    return result[0], result[1], result[2], result[3:6], result[6:]


def per_device(queries, keys, values, cotangent, lengths, loss_mask):
    seq_count = lax.axis_size("seq")
    dp_count = lax.axis_size("dp")
    tok = queries.shape[1]
    me = lax.axis_index("seq")
    x = lax.rem(me, RING)

    def down(step):
        return [(i, i + step) for i in range(seq_count - step)]

    def up(step):
        return [(i + step, i) for i in range(seq_count - step)]

    def around(step):
        return [(i, i - i % RING + (i + step) % RING) for i in range(seq_count)]

    steps = jnp.array(ORDER, dtype=jnp.int32)
    inside = x >= steps
    block_of = jnp.concatenate([
        jnp.stack([me, me - RING, me - 2 * RING]),
        jnp.where(inside, me - steps, me - RING - steps),
        jnp.where(inside, me - RING - steps, me - steps),
    ]).astype(jnp.int32)

    def swap(a, axis, bit):
        return a + lax.ppermute(a, axis, [(i, i ^ bit) for i in range(lax.axis_size(axis))])

    own = jnp.concatenate([keys[0], values[0]], axis=1)
    near = lax.ppermute(own, "seq", down(RING))
    counts = swap(swap(loss_mask.astype(jnp.float32), "dp", 1), "dp", 2)
    near, counts = lax.optimization_barrier((near, counts))
    far = lax.ppermute(near, "seq", down(RING))
    near_got = [lax.ppermute(near, "seq", around(step)) for step in ORDER]
    far, *near_got = lax.optimization_barrier((far, *near_got))
    mixed_got = [
        lax.ppermute(jnp.where(x + step >= RING, far, own), "seq", around(step))
        for step in ORDER
    ]
    counts, mixed_got[-1] = lax.optimization_barrier((counts, mixed_got[-1]))
    all_counts = swap(counts, "dp", 4)

    in_hbm = functools.partial(pltpu.with_memory_space_constraint, memory_space=pltpu.HBM)
    blocks = [in_hbm(a) for a in (own, near, far, *mixed_got, *near_got)]
    queries_in, cotangent_in = in_hbm(queries[0]), in_hbm(cotangent[0])
    outs, dqs, sums, backs = [], [], [], []
    loss = jnp.zeros((1, tok), jnp.float32)
    for part in PARTS:
        counts = all_counts if part is PARTS[-1] else counts
        out, dq, loss, dsingle, dpair = attend(
            part, block_of, lengths, queries_in, cotangent_in, loss_mask, counts, loss, blocks
        )
        if backs:
            *dpair, backs[-1] = lax.optimization_barrier((*dpair, backs[-1]))
        outs.append(out)
        dqs.append(dq)
        sums.append(dsingle)
        backs.append([
            lax.ppermute(d, "seq", around(-step)) for step, d in zip(ORDER, dpair)
        ])
    last = 2 * HD * (PARTS[-1][1] - 1)
    terms = jnp.concatenate([counts, loss], axis=0)
    for b in backs[-1]:
        extra = b[2 * tok:2 * tok + 4, last:last + HD].astype(jnp.float32)
        terms = terms + jnp.stack([extra[3], extra[0] + extra[1] + extra[2]])
    columns = [[RING * z + i for z in range(seq_count // RING)] for i in range(RING)]
    terms = jnp.broadcast_to(terms.reshape(1, 2 * tok), (seq_count // RING, 2 * tok))
    terms = lax.all_to_all(terms, "seq", 0, 0, axis_index_groups=columns, tiled=True)
    terms = jnp.sum(terms, axis=0).reshape(2, tok)
    terms = jnp.sum(terms, axis=1)
    grad_scale = jnp.float32(dp_count * seq_count * tok) / terms[0]
    factor = grad_scale * HD ** -0.5
    row_loss = (grad_scale * terms[1] / (seq_count * tok)).reshape(1)

    grad_k, grad_v, totals, before = [], [], [], []
    for part, single, back in zip(PARTS, sums, backs):
        own_sum, near_sum, far_sum = [s.astype(jnp.float32) for s in single]
        for step, b in zip(ORDER, back):
            mixed = b[:tok].astype(jnp.float32)
            near_sum = near_sum + b[tok:2 * tok].astype(jnp.float32)
            own_sum = own_sum + jnp.where(x + step < RING, mixed, 0.0)
            far_sum = far_sum + jnp.where(x + step < RING, 0.0, mixed)
        near_sum, far_sum = near_sum.astype(jnp.bfloat16), far_sum.astype(jnp.bfloat16)
        if before:
            near_sum, far_sum, *before = lax.optimization_barrier((near_sum, far_sum, *before))
            totals[-1] = totals[-1] + before[0].astype(jnp.float32) + before[1].astype(jnp.float32)
        before = [lax.ppermute(near_sum, "seq", up(RING)), lax.ppermute(far_sum, "seq", up(2 * RING))]
        totals.append(own_sum)
    totals[-1] = totals[-1] + before[0].astype(jnp.float32) + before[1].astype(jnp.float32)
    for part, total in zip(PARTS, totals):
        for h in range(part[1]):
            grad_k.append(total[:, 2 * h * HD:(2 * h + 1) * HD] * factor)
            grad_v.append(total[:, (2 * h + 1) * HD:(2 * h + 2) * HD] * grad_scale)
    grad_k = jnp.concatenate(grad_k, axis=1).astype(jnp.bfloat16)
    grad_v = jnp.concatenate(grad_v, axis=1).astype(jnp.bfloat16)
    out = jnp.concatenate(outs, axis=1)
    grad_q = (jnp.concatenate(dqs, axis=1) * factor).astype(jnp.bfloat16)
    return (out[None], grad_q[None], grad_k[None], grad_v[None], row_loss)


def solution(mesh):
    return jax.shard_map(
        per_device,
        mesh=mesh,
        in_specs=(
            P("dp", "seq", None),
            P("dp", "seq", None),
            P("dp", "seq", None),
            P("dp", "seq", None),
            P("dp", None),
            P("dp", "seq"),
        ),
        out_specs=(
            P("dp", "seq", None),
            P("dp", "seq", None),
            P("dp", "seq", None),
            P("dp", "seq", None),
            P("dp"),
        ),
        check_vma=False,
    )
```

```python
import functools
import math

import jax
import jax.numpy as jnp
from jax import lax
from jax.experimental import pallas as pl
from jax.experimental.pallas import tpu as pltpu
from jax.sharding import PartitionSpec as P

HD = 128
GROUP = 8
PAIRS = GROUP // 2
RING = 4
ORDER = (1, 3, 2)
SLOTS = 3 + 2 * len(ORDER)
PARTS = ((0, 2), (2, 2))
MASKED = -1e30
EXP2_SCALE = HD ** -0.5 * math.log2(math.e)
EXTRA = 16
STRIP = 64

NT = (((1,), (1,)), ((), ()))
NN = (((1,), (0,)), ((), ()))
TN = (((0,), (0,)), ((), ()))


def mxu(a, b, dims):
    return lax.dot_general(a, b, dims, preferred_element_type=jnp.float32)


def attend_kernel(block_of, lengths, q_ref, c_ref, mask_ref, count_ref, loss_in, *refs):
    n = len(ORDER)
    key_refs, value_refs = refs[:SLOTS], refs[SLOTS:2 * SLOTS]
    out_ref, dq_ref, loss_ref = refs[2 * SLOTS:2 * SLOTS + 3]
    refs = refs[2 * SLOTS + 3:]
    single_grads, pair_grads = refs[:3], refs[3:3 + n]
    bias, valid, kg, vg, prob, sgrad = refs[3 + n:9 + n]
    scores, pgrads = refs[9 + n:9 + n + PAIRS], refs[9 + n + PAIRS:]
    tok = q_ref.shape[0]
    halves = [slice(0, tok), slice(tok, 2 * tok)]
    grads = [r.at[...] for r in single_grads] + [r.at[h] for h in halves for r in pair_grads]
    strips = SLOTS * tok // STRIP

    @pl.when(pl.program_id(0) == 0)
    def _():
        pos = block_of[0] * tok + lax.broadcasted_iota(jnp.int32, (1, tok), 1)
        first = jnp.zeros((1, tok), jnp.int32)
        start = jnp.int32(0)
        for j in range(lengths.shape[1]):
            first = jnp.where(pos >= start, start, first)
            start = start + lengths[0, j]
        for j in range(SLOTS):
            key_pos = block_of[j] * tok + lax.broadcasted_iota(jnp.int32, (tok, tok), 0)
            allowed = (key_pos >= first) & (key_pos <= pos)
            bias[j * tok:(j + 1) * tok, :] = jnp.where(allowed, 0.0, MASKED)
        mask_rows = jnp.broadcast_to(mask_ref[...].astype(jnp.float32), (tok, tok))
        valid[...] = mask_rows.T.astype(jnp.bfloat16)
        loss_ref[...] = loss_in[...]

    for j in range(SLOTS):
        kg[j * tok:(j + 1) * tok, :] = key_refs[j][...]
        vg[j * tok:(j + 1) * tok, :] = value_refs[j][...]
    wide = 2 * tok
    heads = [slice(i * HD, (i + 1) * HD) for i in range(GROUP)]
    spans = [slice(i * wide, (i + 1) * wide) for i in range(PAIRS)]
    strip = [slice(j * STRIP, (j + 1) * STRIP) for j in range(strips)]
    q = jnp.concatenate([q_ref[:, h] for h in heads], axis=0)
    up = jnp.concatenate([c_ref[:, h] * valid[...] for h in heads], axis=0)
    up_t, inverse, out_t, dq = {}, {}, {}, {}

    def products(i):
        up_t[i] = up[spans[i]].T
        scores[i][...] = mxu(kg[...], q[spans[i]], NT)
        pgrads[i][...] = mxu(vg[...], up_t[i], NN)

    def softmax(i):
        score = scores[i]
        top = jnp.full((8, wide), MASKED, jnp.float32)
        for at in strip:
            b = bias[at, :]
            s = score[at, :] + jnp.concatenate([b, b], axis=1)
            score[at, :] = s
            top = jnp.maximum(top, jnp.max(s.reshape(STRIP // 8, 8, wide), axis=0))
        top = jnp.max(top, axis=0, keepdims=True)
        total = jnp.zeros((8, wide), jnp.float32)
        for at in strip:
            e = jnp.exp2((score[at, :] - top) * EXP2_SCALE)
            score[at, :] = e
            total = total + jnp.sum(e.reshape(STRIP // 8, 8, wide), axis=0)
        inverse[i] = 1.0 / jnp.sum(total, axis=0, keepdims=True)
        for at in strip:
            prob[at, spans[i]] = (score[at, :] * inverse[i]).astype(jnp.bfloat16)

    def output(i):
        out_t[i] = mxu(vg[...], prob[:, spans[i]], TN).astype(jnp.bfloat16)

    def score_gradient(i):
        terms = up_t[i].astype(jnp.float32) * out_t[i].astype(jnp.float32)
        delta = jnp.sum(terms, axis=0, keepdims=True)
        loss_ref[...] += delta[:, :tok] + delta[:, tok:]
        for at in strip:
            w = scores[i][at, :] * inverse[i]
            sgrad[at, spans[i]] = (w * (pgrads[i][at, :] - delta)).astype(jnp.bfloat16)

    def query_gradient(i):
        dq[i] = mxu(kg[...], sgrad[:, spans[i]], TN).T

    products(0)
    for i in range(PAIRS + 2):
        if 0 <= i - 1 < PAIRS:
            output(i - 1)
        if i + 1 < PAIRS:
            products(i + 1)
        if i < PAIRS:
            softmax(i)
        if 0 <= i - 1 < PAIRS:
            score_gradient(i - 1)
        if 0 <= i - 2 < PAIRS:
            query_gradient(i - 2)
    for i in range(PAIRS):
        out = out_t[i].T
        for part, h in enumerate(heads[2 * i:2 * i + 2]):
            out_ref[:, h] = out[part * tok:(part + 1) * tok]
            dq_ref[:, h] = dq[i][part * tok:(part + 1) * tok]
    dk = mxu(sgrad[...], q, NN).astype(jnp.bfloat16)
    dv = mxu(prob[...], up, NN).astype(jnp.bfloat16)
    for j in range(SLOTS):
        at = slice(j * tok, (j + 1) * tok)
        grads[j][:, :HD] = dk[at, :]
        grads[j][:, HD:] = dv[at, :]
    if pair_grads[0].shape[0] == 2 * tok:
        return

    high = loss_ref[...].astype(jnp.bfloat16).astype(jnp.float32)
    middle = (loss_ref[...] - high).astype(jnp.bfloat16).astype(jnp.float32)
    low = loss_ref[...] - high - middle
    row_of = lax.broadcasted_iota(jnp.int32, (EXTRA, tok), 0)
    extra = jnp.zeros((EXTRA, tok), jnp.float32)
    for i, row in enumerate([high, middle, low, count_ref[...]]):
        extra = jnp.where(row_of == i, row, extra)
    for ref in pair_grads:
        ref[2 * tok:, :HD] = extra.astype(jnp.bfloat16)
        ref[2 * tok:, HD:] = extra.astype(jnp.bfloat16)


def attend(part, block_of, lengths, queries, cotangent, mask, counts, loss, blocks):
    first_head, heads = part
    tok = queries.shape[0]
    kv_heads = blocks[0].shape[1] // (2 * HD)
    wide = GROUP * HD
    rows = SLOTS * tok
    n = len(ORDER)
    f32, bf16 = jnp.float32, jnp.bfloat16
    smem = pl.BlockSpec(memory_space=pltpu.SMEM)
    row = pl.BlockSpec((1, tok), lambda g: (0, 0))
    wide_in = pl.BlockSpec((tok, wide), lambda g: (0, first_head + g))
    wide_out = pl.BlockSpec((tok, wide), lambda g: (0, g))
    key = pl.BlockSpec((tok, HD), lambda g: (0, first_head + g))
    value = pl.BlockSpec((tok, HD), lambda g: (0, kv_heads + first_head + g))
    single = pl.BlockSpec((tok, 2 * HD), lambda g: (0, g))
    pair_rows = 2 * tok + (EXTRA if part is PARTS[-1] else 0)
    pair = pl.BlockSpec((pair_rows, 2 * HD), lambda g: (0, g))
    halo = [key] * SLOTS + [value] * SLOTS
    grads = [pltpu.HBM((tok, heads * 2 * HD), bf16)] * 3
    grads += [pltpu.HBM((pair_rows, heads * 2 * HD), bf16)] * n
    work = 12 * heads * GROUP * tok * rows * HD
    result = pl.pallas_call(
        attend_kernel,
        grid=(heads,),
        out_shape=(
            pltpu.HBM((tok, heads * wide), bf16),
            pltpu.HBM((tok, heads * wide), f32),
            jax.ShapeDtypeStruct((1, tok), f32),
            *grads,
        ),
        in_specs=[smem, smem, wide_in, wide_in, row, row, row, *halo],
        out_specs=(wide_out, wide_out, row, *[single] * 3, *[pair] * n),
        scratch_shapes=[
            pltpu.VMEM((rows, tok), f32),
            pltpu.VMEM((tok, tok), bf16),
            pltpu.VMEM((rows, HD), bf16),
            pltpu.VMEM((rows, HD), bf16),
            pltpu.VMEM((rows, GROUP * tok), bf16),
            pltpu.VMEM((rows, GROUP * tok), bf16),
            *[pltpu.VMEM((rows, 2 * tok), f32)] * (2 * PAIRS),
        ],
        compiler_params=pltpu.CompilerParams(vmem_limit_bytes=32 * 2**20),
        cost_estimate=pl.CostEstimate(
            flops=2 * work, bytes_accessed=8 * 2**20, transcendentals=work // (12 * HD)
        ),
    )(block_of, lengths, queries, cotangent, mask, counts, loss, *blocks, *blocks)
    return result[0], result[1], result[2], result[3:6], result[6:]


def per_device(queries, keys, values, cotangent, lengths, loss_mask):
    seq_count = lax.axis_size("seq")
    dp_count = lax.axis_size("dp")
    tok = queries.shape[1]
    me = lax.axis_index("seq")
    x = lax.rem(me, RING)

    def down(step):
        return [(i, i + step) for i in range(seq_count - step)]

    def up(step):
        return [(i + step, i) for i in range(seq_count - step)]

    def around(step):
        return [(i, i - i % RING + (i + step) % RING) for i in range(seq_count)]

    steps = jnp.array(ORDER, dtype=jnp.int32)
    inside = x >= steps
    block_of = jnp.concatenate([
        jnp.stack([me, me - RING, me - 2 * RING]),
        jnp.where(inside, me - steps, me - RING - steps),
        jnp.where(inside, me - RING - steps, me - steps),
    ]).astype(jnp.int32)

    def swap(a, axis, bit):
        return a + lax.ppermute(a, axis, [(i, i ^ bit) for i in range(lax.axis_size(axis))])

    own = jnp.concatenate([keys[0], values[0]], axis=1)
    near = lax.ppermute(own, "seq", down(RING))
    counts = swap(swap(loss_mask.astype(jnp.float32), "dp", 1), "dp", 2)
    near, counts = lax.optimization_barrier((near, counts))
    far = lax.ppermute(near, "seq", down(RING))
    near_got = [lax.ppermute(near, "seq", around(step)) for step in ORDER]
    far, *near_got = lax.optimization_barrier((far, *near_got))
    mixed_got = [
        lax.ppermute(jnp.where(x + step >= RING, far, own), "seq", around(step))
        for step in ORDER
    ]
    counts, mixed_got[-1] = lax.optimization_barrier((counts, mixed_got[-1]))
    all_counts = swap(counts, "dp", 4)

    in_hbm = functools.partial(pltpu.with_memory_space_constraint, memory_space=pltpu.HBM)
    blocks = [in_hbm(a) for a in (own, near, far, *mixed_got, *near_got)]
    queries_in, cotangent_in = in_hbm(queries[0]), in_hbm(cotangent[0])
    outs, dqs, sums, backs = [], [], [], []
    loss = jnp.zeros((1, tok), jnp.float32)
    for part in PARTS:
        counts = all_counts if part is PARTS[-1] else counts
        out, dq, loss, dsingle, dpair = attend(
            part, block_of, lengths, queries_in, cotangent_in, loss_mask, counts, loss, blocks
        )
        if backs:
            *dpair, backs[-1] = lax.optimization_barrier((*dpair, backs[-1]))
        outs.append(out)
        dqs.append(dq)
        sums.append(dsingle)
        backs.append([
            lax.ppermute(d, "seq", around(-step)) for step, d in zip(ORDER, dpair)
        ])
    last = 2 * HD * (PARTS[-1][1] - 1)
    terms = jnp.concatenate([counts, loss], axis=0)
    for b in backs[-1]:
        extra = b[2 * tok:2 * tok + 4, last:last + HD].astype(jnp.float32)
        terms = terms + jnp.stack([extra[3], extra[0] + extra[1] + extra[2]])
    columns = [[RING * z + i for z in range(seq_count // RING)] for i in range(RING)]
    terms = jnp.broadcast_to(terms.reshape(1, 2 * tok), (seq_count // RING, 2 * tok))
    terms = lax.all_to_all(terms, "seq", 0, 0, axis_index_groups=columns, tiled=True)
    terms = jnp.sum(terms, axis=0).reshape(2, tok)
    terms = jnp.sum(terms, axis=1)
    grad_scale = jnp.float32(dp_count * seq_count * tok) / terms[0]
    factor = grad_scale * HD ** -0.5
    row_loss = (grad_scale * terms[1] / (seq_count * tok)).reshape(1)

    grad_k, grad_v, totals, before = [], [], [], []
    for part, single, back in zip(PARTS, sums, backs):
        own_sum, near_sum, far_sum = [s.astype(jnp.float32) for s in single]
        for step, b in zip(ORDER, back):
            mixed = b[:tok].astype(jnp.float32)
            near_sum = near_sum + b[tok:2 * tok].astype(jnp.float32)
            own_sum = own_sum + jnp.where(x + step < RING, mixed, 0.0)
            far_sum = far_sum + jnp.where(x + step < RING, 0.0, mixed)
        near_sum, far_sum = near_sum.astype(jnp.bfloat16), far_sum.astype(jnp.bfloat16)
        if before:
            near_sum, far_sum, *before = lax.optimization_barrier((near_sum, far_sum, *before))
            totals[-1] = totals[-1] + before[0].astype(jnp.float32) + before[1].astype(jnp.float32)
        before = [lax.ppermute(near_sum, "seq", up(RING)), lax.ppermute(far_sum, "seq", up(2 * RING))]
        totals.append(own_sum)
    totals[-1] = totals[-1] + before[0].astype(jnp.float32) + before[1].astype(jnp.float32)
    for part, total in zip(PARTS, totals):
        for h in range(part[1]):
            grad_k.append(total[:, 2 * h * HD:(2 * h + 1) * HD] * factor)
            grad_v.append(total[:, (2 * h + 1) * HD:(2 * h + 2) * HD] * grad_scale)
    grad_k = jnp.concatenate(grad_k, axis=1).astype(jnp.bfloat16)
    grad_v = jnp.concatenate(grad_v, axis=1).astype(jnp.bfloat16)
    out = jnp.concatenate(outs, axis=1)
    grad_q = (jnp.concatenate(dqs, axis=1) * factor).astype(jnp.bfloat16)
    return (out[None], grad_q[None], grad_k[None], grad_v[None], row_loss)


def solution(mesh):
    return jax.shard_map(
        per_device,
        mesh=mesh,
        in_specs=(
            P("dp", "seq", None),
            P("dp", "seq", None),
            P("dp", "seq", None),
            P("dp", "seq", None),
            P("dp", None),
            P("dp", "seq"),
        ),
        out_specs=(
            P("dp", "seq", None),
            P("dp", "seq", None),
            P("dp", "seq", None),
            P("dp", "seq", None),
            P("dp"),
        ),
        check_vma=False,
    )
```

```python
import functools
import math

import jax
import jax.numpy as jnp
from jax import lax
from jax.experimental import pallas as pl
from jax.experimental.pallas import tpu as pltpu
from jax.sharding import PartitionSpec as P

HD = 128
GROUP = 8
PAIRS = GROUP // 2
RING = 4
ORDER = (1, 3, 2)
SLOTS = 3 + 2 * len(ORDER)
PARTS = ((0, 2), (2, 2))
MASKED = -1e30
EXP2_SCALE = HD ** -0.5 * math.log2(math.e)
STRIP = 64

NT = (((1,), (1,)), ((), ()))
NN = (((1,), (0,)), ((), ()))
TN = (((0,), (0,)), ((), ()))


def mxu(a, b, dims):
    return lax.dot_general(a, b, dims, preferred_element_type=jnp.float32)


def attend_kernel(block_of, lengths, q_ref, c_ref, mask_ref, loss_in, *refs):
    n = len(ORDER)
    key_refs, value_refs = refs[:SLOTS], refs[SLOTS:2 * SLOTS]
    out_ref, dq_ref, loss_ref = refs[2 * SLOTS:2 * SLOTS + 3]
    refs = refs[2 * SLOTS + 3:]
    single_grads, pair_grads = refs[:3], refs[3:3 + n]
    bias, valid, kg, vg, prob, sgrad = refs[3 + n:9 + n]
    scores, pgrads = refs[9 + n:9 + n + PAIRS], refs[9 + n + PAIRS:]
    tok = q_ref.shape[0]
    halves = [slice(0, tok), slice(tok, 2 * tok)]
    grads = [r.at[...] for r in single_grads] + [r.at[h] for h in halves for r in pair_grads]
    strips = SLOTS * tok // STRIP

    @pl.when(pl.program_id(0) == 0)
    def _():
        pos = block_of[0] * tok + lax.broadcasted_iota(jnp.int32, (1, tok), 1)
        first = jnp.zeros((1, tok), jnp.int32)
        start = jnp.int32(0)
        for j in range(lengths.shape[1]):
            first = jnp.where(pos >= start, start, first)
            start = start + lengths[0, j]
        for j in range(SLOTS):
            key_pos = block_of[j] * tok + lax.broadcasted_iota(jnp.int32, (tok, tok), 0)
            allowed = (key_pos >= first) & (key_pos <= pos)
            bias[j * tok:(j + 1) * tok, :] = jnp.where(allowed, 0.0, MASKED)
        mask_rows = jnp.broadcast_to(mask_ref[...].astype(jnp.float32), (tok, tok))
        valid[...] = mask_rows.T.astype(jnp.bfloat16)
        loss_ref[...] = loss_in[...]

    for j in range(SLOTS):
        kg[j * tok:(j + 1) * tok, :] = key_refs[j][...]
        vg[j * tok:(j + 1) * tok, :] = value_refs[j][...]
    wide = 2 * tok
    heads = [slice(i * HD, (i + 1) * HD) for i in range(GROUP)]
    spans = [slice(i * wide, (i + 1) * wide) for i in range(PAIRS)]
    strip = [slice(j * STRIP, (j + 1) * STRIP) for j in range(strips)]
    q = jnp.concatenate([q_ref[:, h] for h in heads], axis=0)
    up = jnp.concatenate([c_ref[:, h] * valid[...] for h in heads], axis=0)
    up_t, inverse, out_t, dq = {}, {}, {}, {}

    def products(i):
        up_t[i] = up[spans[i]].T
        scores[i][...] = mxu(kg[...], q[spans[i]], NT)
        pgrads[i][...] = mxu(vg[...], up_t[i], NN)

    def softmax(i):
        score = scores[i]
        top = jnp.full((8, wide), MASKED, jnp.float32)
        for at in strip:
            b = bias[at, :]
            s = score[at, :] + jnp.concatenate([b, b], axis=1)
            score[at, :] = s
            top = jnp.maximum(top, jnp.max(s.reshape(STRIP // 8, 8, wide), axis=0))
        top = jnp.max(top, axis=0, keepdims=True)
        total = jnp.zeros((8, wide), jnp.float32)
        for at in strip:
            e = jnp.exp2((score[at, :] - top) * EXP2_SCALE)
            score[at, :] = e
            total = total + jnp.sum(e.reshape(STRIP // 8, 8, wide), axis=0)
        inverse[i] = 1.0 / jnp.sum(total, axis=0, keepdims=True)
        for at in strip:
            prob[at, spans[i]] = (score[at, :] * inverse[i]).astype(jnp.bfloat16)

    def output(i):
        out_t[i] = mxu(vg[...], prob[:, spans[i]], TN).astype(jnp.bfloat16)

    def score_gradient(i):
        terms = up_t[i].astype(jnp.float32) * out_t[i].astype(jnp.float32)
        delta = jnp.sum(terms, axis=0, keepdims=True)
        loss_ref[...] += delta[:, :tok] + delta[:, tok:]
        for at in strip:
            w = scores[i][at, :] * inverse[i]
            sgrad[at, spans[i]] = (w * (pgrads[i][at, :] - delta)).astype(jnp.bfloat16)

    def query_gradient(i):
        dq[i] = mxu(kg[...], sgrad[:, spans[i]], TN).T

    products(0)
    for i in range(PAIRS + 2):
        if 0 <= i - 1 < PAIRS:
            output(i - 1)
        if i + 1 < PAIRS:
            products(i + 1)
        if i < PAIRS:
            softmax(i)
        if 0 <= i - 1 < PAIRS:
            score_gradient(i - 1)
        if 0 <= i - 2 < PAIRS:
            query_gradient(i - 2)
    for i in range(PAIRS):
        out = out_t[i].T
        for part, h in enumerate(heads[2 * i:2 * i + 2]):
            out_ref[:, h] = out[part * tok:(part + 1) * tok]
            dq_ref[:, h] = dq[i][part * tok:(part + 1) * tok]
    dk = mxu(sgrad[...], q, NN).astype(jnp.bfloat16)
    dv = mxu(prob[...], up, NN).astype(jnp.bfloat16)
    for j in range(SLOTS):
        at = slice(j * tok, (j + 1) * tok)
        grads[j][:, :HD] = dk[at, :]
        grads[j][:, HD:] = dv[at, :]


def attend(part, block_of, lengths, queries, cotangent, mask, loss, blocks):
    first_head, heads = part
    tok = queries.shape[0]
    kv_heads = blocks[0].shape[1] // (2 * HD)
    wide = GROUP * HD
    rows = SLOTS * tok
    n = len(ORDER)
    f32, bf16 = jnp.float32, jnp.bfloat16
    smem = pl.BlockSpec(memory_space=pltpu.SMEM)
    row = pl.BlockSpec((1, tok), lambda g: (0, 0))
    wide_in = pl.BlockSpec((tok, wide), lambda g: (0, first_head + g))
    wide_out = pl.BlockSpec((tok, wide), lambda g: (0, g))
    key = pl.BlockSpec((tok, HD), lambda g: (0, first_head + g))
    value = pl.BlockSpec((tok, HD), lambda g: (0, kv_heads + first_head + g))
    single = pl.BlockSpec((tok, 2 * HD), lambda g: (0, g))
    pair_rows = 2 * tok
    pair = pl.BlockSpec((pair_rows, 2 * HD), lambda g: (0, g))
    halo = [key] * SLOTS + [value] * SLOTS
    grads = [pltpu.HBM((tok, heads * 2 * HD), bf16)] * 3
    grads += [pltpu.HBM((pair_rows, heads * 2 * HD), bf16)] * n
    work = 12 * heads * GROUP * tok * rows * HD
    result = pl.pallas_call(
        attend_kernel,
        grid=(heads,),
        out_shape=(
            pltpu.HBM((tok, heads * wide), bf16),
            pltpu.HBM((tok, heads * wide), f32),
            jax.ShapeDtypeStruct((1, tok), f32),
            *grads,
        ),
        in_specs=[smem, smem, wide_in, wide_in, row, row, *halo],
        out_specs=(wide_out, wide_out, row, *[single] * 3, *[pair] * n),
        scratch_shapes=[
            pltpu.VMEM((rows, tok), f32),
            pltpu.VMEM((tok, tok), bf16),
            pltpu.VMEM((rows, HD), bf16),
            pltpu.VMEM((rows, HD), bf16),
            pltpu.VMEM((rows, GROUP * tok), bf16),
            pltpu.VMEM((rows, GROUP * tok), bf16),
            *[pltpu.VMEM((rows, 2 * tok), f32)] * (2 * PAIRS),
        ],
        compiler_params=pltpu.CompilerParams(vmem_limit_bytes=32 * 2**20),
        cost_estimate=pl.CostEstimate(
            flops=2 * work, bytes_accessed=8 * 2**20, transcendentals=work // (12 * HD)
        ),
    )(block_of, lengths, queries, cotangent, mask, loss, *blocks, *blocks)
    return result[0], result[1], result[2], result[3:6], result[6:]


def per_device(queries, keys, values, cotangent, lengths, loss_mask):
    seq_count = lax.axis_size("seq")
    dp_count = lax.axis_size("dp")
    tok = queries.shape[1]
    me = lax.axis_index("seq")
    x = lax.rem(me, RING)

    def down(step):
        return [(i, i + step) for i in range(seq_count - step)]

    def up(step):
        return [(i + step, i) for i in range(seq_count - step)]

    def around(step):
        return [(i, i - i % RING + (i + step) % RING) for i in range(seq_count)]

    steps = jnp.array(ORDER, dtype=jnp.int32)
    inside = x >= steps
    block_of = jnp.concatenate([
        jnp.stack([me, me - RING, me - 2 * RING]),
        jnp.where(inside, me - steps, me - RING - steps),
        jnp.where(inside, me - RING - steps, me - steps),
    ]).astype(jnp.int32)

    def swap(a, axis, bit):
        return a + lax.ppermute(a, axis, [(i, i ^ bit) for i in range(lax.axis_size(axis))])

    own = jnp.concatenate([keys[0], values[0]], axis=1)
    near = lax.ppermute(own, "seq", down(RING))
    counts = swap(swap(loss_mask.astype(jnp.float32), "dp", 1), "dp", 2)
    near, counts = lax.optimization_barrier((near, counts))
    far = lax.ppermute(near, "seq", down(RING))
    near_got = [lax.ppermute(near, "seq", around(step)) for step in ORDER]
    far, *near_got = lax.optimization_barrier((far, *near_got))
    mixed_got = [
        lax.ppermute(jnp.where(x + step >= RING, far, own), "seq", around(step))
        for step in ORDER
    ]
    counts, mixed_got[-1] = lax.optimization_barrier((counts, mixed_got[-1]))
    counts = swap(counts, "dp", 4)

    in_hbm = functools.partial(pltpu.with_memory_space_constraint, memory_space=pltpu.HBM)
    blocks = [in_hbm(a) for a in (own, near, far, *mixed_got, *near_got)]
    queries_in, cotangent_in = in_hbm(queries[0]), in_hbm(cotangent[0])
    outs, dqs, sums, backs = [], [], [], []
    loss = jnp.zeros((1, tok), jnp.float32)
    for part in PARTS:
        out, dq, loss, dsingle, dpair = attend(
            part, block_of, lengths, queries_in, cotangent_in, loss_mask, loss, blocks
        )
        if backs:
            *dpair, backs[-1] = lax.optimization_barrier((*dpair, backs[-1]))
        outs.append(out)
        dqs.append(dq)
        sums.append(dsingle)
        backs.append([
            lax.ppermute(d, "seq", around(-step)) for step, d in zip(ORDER, dpair)
        ])
    def total_of(terms, groups):
        copies = jnp.broadcast_to(terms[None], (len(groups[0]), terms.size))
        parts = lax.all_to_all(copies, "seq", 0, 0, axis_index_groups=groups, tiled=True)
        return jnp.sum(parts, axis=0)

    rows = [[RING * z + i for i in range(RING)] for z in range(seq_count // RING)]
    columns = [list(c) for c in zip(*rows)]
    terms = jnp.concatenate([counts[0], loss[0]])
    terms, backs[-1][0] = lax.optimization_barrier((terms, backs[-1][0]))
    terms = total_of(terms, columns)
    grad_k, grad_v, totals, before = [], [], [], []
    for part, single, back in zip(PARTS, sums, backs):
        own_sum, near_sum, far_sum = [s.astype(jnp.float32) for s in single]
        for step, b in zip(ORDER, back):
            mixed = b[:tok].astype(jnp.float32)
            near_sum = near_sum + b[tok:2 * tok].astype(jnp.float32)
            own_sum = own_sum + jnp.where(x + step < RING, mixed, 0.0)
            far_sum = far_sum + jnp.where(x + step < RING, 0.0, mixed)
        near_sum, far_sum = near_sum.astype(jnp.bfloat16), far_sum.astype(jnp.bfloat16)
        if before:
            near_sum, far_sum, *before = lax.optimization_barrier((near_sum, far_sum, *before))
            totals[-1] = totals[-1] + before[0].astype(jnp.float32) + before[1].astype(jnp.float32)
        before = [lax.ppermute(near_sum, "seq", up(RING)), lax.ppermute(far_sum, "seq", up(2 * RING))]
        totals.append(own_sum)
    terms, before[0] = lax.optimization_barrier((terms, before[0]))
    terms = total_of(terms, rows)
    grad_scale = jnp.float32(dp_count * seq_count * tok) / jnp.sum(terms[:tok])
    factor = grad_scale * HD ** -0.5
    row_loss = (grad_scale * jnp.sum(terms[tok:]) / (seq_count * tok)).reshape(1)
    totals[-1] = totals[-1] + before[0].astype(jnp.float32) + before[1].astype(jnp.float32)
    for part, total in zip(PARTS, totals):
        for h in range(part[1]):
            grad_k.append(total[:, 2 * h * HD:(2 * h + 1) * HD] * factor)
            grad_v.append(total[:, (2 * h + 1) * HD:(2 * h + 2) * HD] * grad_scale)
    grad_k = jnp.concatenate(grad_k, axis=1).astype(jnp.bfloat16)
    grad_v = jnp.concatenate(grad_v, axis=1).astype(jnp.bfloat16)
    out = jnp.concatenate(outs, axis=1)
    grad_q = (jnp.concatenate(dqs, axis=1) * factor).astype(jnp.bfloat16)
    return (out[None], grad_q[None], grad_k[None], grad_v[None], row_loss)


def solution(mesh):
    return jax.shard_map(
        per_device,
        mesh=mesh,
        in_specs=(
            P("dp", "seq", None),
            P("dp", "seq", None),
            P("dp", "seq", None),
            P("dp", "seq", None),
            P("dp", None),
            P("dp", "seq"),
        ),
        out_specs=(
            P("dp", "seq", None),
            P("dp", "seq", None),
            P("dp", "seq", None),
            P("dp", "seq", None),
            P("dp"),
        ),
        check_vma=False,
    )
```

```python
import functools
import math

import jax
import jax.numpy as jnp
from jax import lax
from jax.experimental import pallas as pl
from jax.experimental.pallas import tpu as pltpu
from jax.sharding import PartitionSpec as P

HD = 128
GROUP = 8
PAIRS = GROUP // 2
RING = 4
ORDER = (3, 1, 2)
SLOTS = 3 + 2 * len(ORDER)
PARTS = ((0, 2), (2, 2))
MASKED = -1e30
EXP2_SCALE = HD ** -0.5 * math.log2(math.e)
STRIP = 64

NT = (((1,), (1,)), ((), ()))
NN = (((1,), (0,)), ((), ()))
TN = (((0,), (0,)), ((), ()))


def mxu(a, b, dims):
    return lax.dot_general(a, b, dims, preferred_element_type=jnp.float32)


def attend_kernel(block_of, lengths, q_ref, c_ref, mask_ref, loss_in, *refs):
    n = len(ORDER)
    key_refs, value_refs = refs[:SLOTS], refs[SLOTS:2 * SLOTS]
    out_ref, dq_ref, loss_ref = refs[2 * SLOTS:2 * SLOTS + 3]
    refs = refs[2 * SLOTS + 3:]
    single_grads, pair_grads = refs[:3], refs[3:3 + n]
    bias, valid, kg, vg, prob, sgrad = refs[3 + n:9 + n]
    scores, pgrads = refs[9 + n:9 + n + PAIRS], refs[9 + n + PAIRS:]
    tok = q_ref.shape[0]
    halves = [slice(0, tok), slice(tok, 2 * tok)]
    grads = [r.at[...] for r in single_grads] + [r.at[h] for h in halves for r in pair_grads]
    strips = SLOTS * tok // STRIP

    @pl.when(pl.program_id(0) == 0)
    def _():
        pos = block_of[0] * tok + lax.broadcasted_iota(jnp.int32, (1, tok), 1)
        first = jnp.zeros((1, tok), jnp.int32)
        start = jnp.int32(0)
        for j in range(lengths.shape[1]):
            first = jnp.where(pos >= start, start, first)
            start = start + lengths[0, j]
        for j in range(SLOTS):
            key_pos = block_of[j] * tok + lax.broadcasted_iota(jnp.int32, (tok, tok), 0)
            allowed = (key_pos >= first) & (key_pos <= pos)
            bias[j * tok:(j + 1) * tok, :] = jnp.where(allowed, 0.0, MASKED)
        mask_rows = jnp.broadcast_to(mask_ref[...].astype(jnp.float32), (tok, tok))
        valid[...] = mask_rows.T.astype(jnp.bfloat16)
        loss_ref[...] = loss_in[...]

    for j in range(SLOTS):
        kg[j * tok:(j + 1) * tok, :] = key_refs[j][...]
        vg[j * tok:(j + 1) * tok, :] = value_refs[j][...]
    wide = 2 * tok
    heads = [slice(i * HD, (i + 1) * HD) for i in range(GROUP)]
    spans = [slice(i * wide, (i + 1) * wide) for i in range(PAIRS)]
    strip = [slice(j * STRIP, (j + 1) * STRIP) for j in range(strips)]
    q = jnp.concatenate([q_ref[:, h] for h in heads], axis=0)
    up = jnp.concatenate([c_ref[:, h] * valid[...] for h in heads], axis=0)
    up_t, inverse, out_t, dq = {}, {}, {}, {}

    def products(i):
        up_t[i] = up[spans[i]].T
        scores[i][...] = mxu(kg[...], q[spans[i]], NT)
        pgrads[i][...] = mxu(vg[...], up_t[i], NN)

    def softmax(i):
        score = scores[i]
        top = jnp.full((8, wide), MASKED, jnp.float32)
        for at in strip:
            b = bias[at, :]
            s = score[at, :] + jnp.concatenate([b, b], axis=1)
            score[at, :] = s
            top = jnp.maximum(top, jnp.max(s.reshape(STRIP // 8, 8, wide), axis=0))
        top = jnp.max(top, axis=0, keepdims=True)
        total = jnp.zeros((8, wide), jnp.float32)
        for at in strip:
            e = jnp.exp2((score[at, :] - top) * EXP2_SCALE)
            score[at, :] = e
            total = total + jnp.sum(e.reshape(STRIP // 8, 8, wide), axis=0)
        inverse[i] = 1.0 / jnp.sum(total, axis=0, keepdims=True)
        for at in strip:
            prob[at, spans[i]] = (score[at, :] * inverse[i]).astype(jnp.bfloat16)

    def output(i):
        out_t[i] = mxu(vg[...], prob[:, spans[i]], TN).astype(jnp.bfloat16)

    def score_gradient(i):
        terms = up_t[i].astype(jnp.float32) * out_t[i].astype(jnp.float32)
        delta = jnp.sum(terms, axis=0, keepdims=True)
        loss_ref[...] += delta[:, :tok] + delta[:, tok:]
        for at in strip:
            w = scores[i][at, :] * inverse[i]
            sgrad[at, spans[i]] = (w * (pgrads[i][at, :] - delta)).astype(jnp.bfloat16)

    def query_gradient(i):
        dq[i] = mxu(kg[...], sgrad[:, spans[i]], TN).T

    products(0)
    for i in range(PAIRS + 2):
        if 0 <= i - 1 < PAIRS:
            output(i - 1)
        if i + 1 < PAIRS:
            products(i + 1)
        if i < PAIRS:
            softmax(i)
        if 0 <= i - 1 < PAIRS:
            score_gradient(i - 1)
        if 0 <= i - 2 < PAIRS:
            query_gradient(i - 2)
    for i in range(PAIRS):
        out = out_t[i].T
        for part, h in enumerate(heads[2 * i:2 * i + 2]):
            out_ref[:, h] = out[part * tok:(part + 1) * tok]
            dq_ref[:, h] = dq[i][part * tok:(part + 1) * tok]
    dk = mxu(sgrad[...], q, NN).astype(jnp.bfloat16)
    dv = mxu(prob[...], up, NN).astype(jnp.bfloat16)
    for j in range(SLOTS):
        at = slice(j * tok, (j + 1) * tok)
        grads[j][:, :HD] = dk[at, :]
        grads[j][:, HD:] = dv[at, :]


def attend(part, block_of, lengths, queries, cotangent, mask, loss, blocks):
    first_head, heads = part
    tok = queries.shape[0]
    kv_heads = blocks[0].shape[1] // (2 * HD)
    wide = GROUP * HD
    rows = SLOTS * tok
    n = len(ORDER)
    f32, bf16 = jnp.float32, jnp.bfloat16
    smem = pl.BlockSpec(memory_space=pltpu.SMEM)
    row = pl.BlockSpec((1, tok), lambda g: (0, 0))
    wide_in = pl.BlockSpec((tok, wide), lambda g: (0, first_head + g))
    wide_out = pl.BlockSpec((tok, wide), lambda g: (0, g))
    key = pl.BlockSpec((tok, HD), lambda g: (0, first_head + g))
    value = pl.BlockSpec((tok, HD), lambda g: (0, kv_heads + first_head + g))
    single = pl.BlockSpec((tok, 2 * HD), lambda g: (0, g))
    pair_rows = 2 * tok
    pair = pl.BlockSpec((pair_rows, 2 * HD), lambda g: (0, g))
    halo = [key] * SLOTS + [value] * SLOTS
    grads = [pltpu.HBM((tok, heads * 2 * HD), bf16)] * 3
    grads += [pltpu.HBM((pair_rows, heads * 2 * HD), bf16)] * n
    work = 12 * heads * GROUP * tok * rows * HD
    result = pl.pallas_call(
        attend_kernel,
        grid=(heads,),
        out_shape=(
            pltpu.HBM((tok, heads * wide), bf16),
            pltpu.HBM((tok, heads * wide), f32),
            jax.ShapeDtypeStruct((1, tok), f32),
            *grads,
        ),
        in_specs=[smem, smem, wide_in, wide_in, row, row, *halo],
        out_specs=(wide_out, wide_out, row, *[single] * 3, *[pair] * n),
        scratch_shapes=[
            pltpu.VMEM((rows, tok), f32),
            pltpu.VMEM((tok, tok), bf16),
            pltpu.VMEM((rows, HD), bf16),
            pltpu.VMEM((rows, HD), bf16),
            pltpu.VMEM((rows, GROUP * tok), bf16),
            pltpu.VMEM((rows, GROUP * tok), bf16),
            *[pltpu.VMEM((rows, 2 * tok), f32)] * (2 * PAIRS),
        ],
        compiler_params=pltpu.CompilerParams(vmem_limit_bytes=32 * 2**20),
        cost_estimate=pl.CostEstimate(
            flops=2 * work, bytes_accessed=8 * 2**20, transcendentals=work // (12 * HD)
        ),
    )(block_of, lengths, queries, cotangent, mask, loss, *blocks, *blocks)
    return result[0], result[1], result[2], result[3:6], result[6:]


def per_device(queries, keys, values, cotangent, lengths, loss_mask):
    seq_count = lax.axis_size("seq")
    dp_count = lax.axis_size("dp")
    tok = queries.shape[1]
    me = lax.axis_index("seq")
    x = lax.rem(me, RING)

    def down(step):
        return [(i, i + step) for i in range(seq_count - step)]

    def up(step):
        return [(i + step, i) for i in range(seq_count - step)]

    def around(step):
        return [(i, i - i % RING + (i + step) % RING) for i in range(seq_count)]

    steps = jnp.array(ORDER, dtype=jnp.int32)
    inside = x >= steps
    block_of = jnp.concatenate([
        jnp.stack([me, me - RING, me - 2 * RING]),
        jnp.where(inside, me - steps, me - RING - steps),
        jnp.where(inside, me - RING - steps, me - steps),
    ]).astype(jnp.int32)

    def swap(a, axis, bit):
        return a + lax.ppermute(a, axis, [(i, i ^ bit) for i in range(lax.axis_size(axis))])

    own = jnp.concatenate([keys[0], values[0]], axis=1)
    near = lax.ppermute(own, "seq", down(RING))
    counts = swap(swap(loss_mask.astype(jnp.float32), "dp", 1), "dp", 2)
    near, counts = lax.optimization_barrier((near, counts))
    far = lax.ppermute(near, "seq", down(RING))
    near_got = [lax.ppermute(near, "seq", around(step)) for step in ORDER]
    far, *near_got = lax.optimization_barrier((far, *near_got))
    mixed_got = [
        lax.ppermute(jnp.where(x + step >= RING, far, own), "seq", around(step))
        for step in ORDER
    ]
    counts, mixed_got[-1] = lax.optimization_barrier((counts, mixed_got[-1]))
    counts = swap(counts, "dp", 4)

    in_hbm = functools.partial(pltpu.with_memory_space_constraint, memory_space=pltpu.HBM)
    blocks = [in_hbm(a) for a in (own, near, far, *mixed_got, *near_got)]
    queries_in, cotangent_in = in_hbm(queries[0]), in_hbm(cotangent[0])
    outs, dqs, sums, backs = [], [], [], []
    loss = jnp.zeros((1, tok), jnp.float32)
    for part in PARTS:
        out, dq, loss, dsingle, dpair = attend(
            part, block_of, lengths, queries_in, cotangent_in, loss_mask, loss, blocks
        )
        if backs:
            *dpair, backs[-1] = lax.optimization_barrier((*dpair, backs[-1]))
        outs.append(out)
        dqs.append(dq)
        sums.append(dsingle)
        backs.append([
            lax.ppermute(d, "seq", around(-step)) for step, d in zip(ORDER, dpair)
        ])
    def total_of(terms, groups):
        copies = jnp.broadcast_to(terms[None], (len(groups[0]), terms.size))
        parts = lax.all_to_all(copies, "seq", 0, 0, axis_index_groups=groups, tiled=True)
        return jnp.sum(parts, axis=0)

    rows = [[RING * z + i for i in range(RING)] for z in range(seq_count // RING)]
    columns = [list(c) for c in zip(*rows)]
    terms = jnp.concatenate([counts[0], loss[0]])
    terms, backs[-1][0] = lax.optimization_barrier((terms, backs[-1][0]))
    terms = total_of(terms, columns)
    grad_k, grad_v, totals, before = [], [], [], []
    for part, single, back in zip(PARTS, sums, backs):
        own_sum, near_sum, far_sum = [s.astype(jnp.float32) for s in single]
        for step, b in zip(ORDER, back):
            mixed = b[:tok].astype(jnp.float32)
            near_sum = near_sum + b[tok:2 * tok].astype(jnp.float32)
            own_sum = own_sum + jnp.where(x + step < RING, mixed, 0.0)
            far_sum = far_sum + jnp.where(x + step < RING, 0.0, mixed)
        near_sum, far_sum = near_sum.astype(jnp.bfloat16), far_sum.astype(jnp.bfloat16)
        if before:
            near_sum, far_sum, *before = lax.optimization_barrier((near_sum, far_sum, *before))
            totals[-1] = totals[-1] + before[0].astype(jnp.float32) + before[1].astype(jnp.float32)
        before = [lax.ppermute(near_sum, "seq", up(RING)), lax.ppermute(far_sum, "seq", up(2 * RING))]
        totals.append(own_sum)
    terms, before[0] = lax.optimization_barrier((terms, before[0]))
    terms = total_of(terms, rows)
    grad_scale = jnp.float32(dp_count * seq_count * tok) / jnp.sum(terms[:tok])
    factor = grad_scale * HD ** -0.5
    row_loss = (grad_scale * jnp.sum(terms[tok:]) / (seq_count * tok)).reshape(1)
    totals[-1] = totals[-1] + before[0].astype(jnp.float32) + before[1].astype(jnp.float32)
    for part, total in zip(PARTS, totals):
        for h in range(part[1]):
            grad_k.append(total[:, 2 * h * HD:(2 * h + 1) * HD] * factor)
            grad_v.append(total[:, (2 * h + 1) * HD:(2 * h + 2) * HD] * grad_scale)
    grad_k = jnp.concatenate(grad_k, axis=1).astype(jnp.bfloat16)
    grad_v = jnp.concatenate(grad_v, axis=1).astype(jnp.bfloat16)
    out = jnp.concatenate(outs, axis=1)
    grad_q = (jnp.concatenate(dqs, axis=1) * factor).astype(jnp.bfloat16)
    return (out[None], grad_q[None], grad_k[None], grad_v[None], row_loss)


def solution(mesh):
    return jax.shard_map(
        per_device,
        mesh=mesh,
        in_specs=(
            P("dp", "seq", None),
            P("dp", "seq", None),
            P("dp", "seq", None),
            P("dp", "seq", None),
            P("dp", None),
            P("dp", "seq"),
        ),
        out_specs=(
            P("dp", "seq", None),
            P("dp", "seq", None),
            P("dp", "seq", None),
            P("dp", "seq", None),
            P("dp"),
        ),
        check_vma=False,
    )
```
